256 devices in a mesh: dp: 16 (over x, y), zero: 16 (over z, core).
Axes of the slice: x: 4, y: 4, z: 8, core: 2. Of those that a mesh axis runs over, the one named last changes fastest.
Arguments:
- gradients: bfloat16 [16, 16, 384, 4096], P('dp', None, None, 'zero'), may hold values from -6 to 6
- momentum: bfloat16 [16, 384, 4096], P(None, None, 'zero'), may hold values from -6 to 6
- bucket_slot: int32 [16], replicated, may hold values from 0 to 15, each once
Outputs:
- new_moment: bfloat16 [16, 384, 4096], P(None, None, 'zero')
- update: bfloat16 [16, 384, 4096], P(None, None, 'zero')
The draws below stay inside these ranges and needn't reach their ends.
Inputs may be any that keep to these rules, and one draw needn't show every extreme that they name: bucket_slot is a permutation of 0 to 15.
All inputs are finite; a program needn't handle non-finite values.
Results may differ from the reference program's by a relative error of at most 0.04.
Values may be sent and summed in bfloat16 or wider, within the bound.
No kernel may reach another device: no remote copies, remote signals or barrier semaphores. Data moves between devices by JAX's collectives and lax.ppermute only.
A program may use at most 128 MiB of HBM per device.

```python
import math
import jax
import jax.numpy as jnp
from jax import lax

D = 4096
ROWS = 384
ITERS = 5
MATS = 16
N_DP = 16


def block_scale(own_key, dims, pieces, low, largest):
    def one(dim, parts):
        draws = jax.random.uniform(jax.random.fold_in(jax.random.fold_in(own_key, 6), dim), (parts,), jnp.float32, low / len(pieces), largest / len(pieces))
        return jnp.repeat(jnp.exp(draws), dims[dim] // parts).reshape((-1,) + (1,) * (len(dims) - dim - 1))

    gain = one(*pieces[0])
    for cut in pieces[1:]:
        gain = gain * one(*cut)
    return gain


def noise(rng, shape, width, most, cuts=(), held_as=jnp.bfloat16):
    factor_of = block_scale(rng, shape, cuts, -0.22, 0.18) if cuts else 1.0
    result = jax.random.normal(rng, shape, jnp.float32) * width * factor_of
    return jnp.minimum(jnp.maximum(result, -most), most).astype(held_as)


def setup_inputs(seed: int = 0) -> dict:
    keys = jax.random.split(jax.random.key(seed), 4)
    return {
        "gradients": noise(keys[0], (N_DP, MATS, ROWS, D), 1.0, 6.0, ((0, 16), (3, 16))),
        "momentum": noise(keys[1], (MATS, ROWS, D), 1.0, 6.0, ((2, 16),)),
        "bucket_slot": jax.random.permutation(keys[2], MATS).astype(jnp.int32),
    }


momentum_decay = 0.95
coef_first = 3.4445
coef_second = -4.775
coef_third = 2.0315
rms_factor = 0.2
tiny_value = 1e-07

def orthogonal_step(direction):
    values = direction.astype(jnp.float32)
    norm_total = jnp.sqrt(jnp.sum(values * values))
    iterate = (values / (norm_total + tiny_value)).astype(jnp.bfloat16)
    for repeat in range(ITERS):
        gram_matrix = lax.dot_general(iterate, iterate, (((1,), (1,)), ((), ())), preferred_element_type=jnp.float32).astype(jnp.bfloat16)
        square = jnp.dot(gram_matrix, gram_matrix, preferred_element_type=jnp.float32)
        polynomial = (coef_second * gram_matrix.astype(jnp.float32) + coef_third * square).astype(jnp.bfloat16)
        iterate = (coef_first * iterate.astype(jnp.float32) + jnp.dot(polynomial, iterate, preferred_element_type=jnp.float32)).astype(jnp.bfloat16)
    factor = rms_factor * math.sqrt(max(ROWS, D))
    return (factor * iterate.astype(jnp.float32)).astype(jnp.bfloat16)

def reference(gradients, momentum, bucket_slot):
    summed = lax.optimization_barrier(jnp.sum(gradients, axis=0, dtype=jnp.float32))
    average = jnp.take(summed, bucket_slot.astype(jnp.int32), axis=0) / N_DP
    new_moment = (momentum_decay * momentum.astype(jnp.float32) + average).astype(jnp.bfloat16)
    direction = (average + momentum_decay * new_moment.astype(jnp.float32)).astype(jnp.bfloat16)
    update = lax.map(orthogonal_step, direction)
    return (new_moment, update)
```

```python
import functools
import math

import jax
import jax.numpy as jnp
from jax import lax
from jax.experimental import pallas as pl
from jax.experimental.pallas import tpu as pltpu
from jax.sharding import PartitionSpec as P

D = 4096
ROWS = 384
ITERS = 5

momentum_decay = 0.95
coef_first = 3.4445
coef_second = -4.775
coef_third = 2.0315
rms_factor = 0.2
tiny_value = 1e-07

BF16 = jnp.bfloat16
F32 = jnp.float32
SIDE = 4
HALF = ROWS // 2


def gray(position):
    return position ^ (position >> 1)


def all_pairs(mesh_sizes, target):
    replicas, owners = mesh_sizes
    pairs = []
    for dp in range(replicas):
        for zero in range(owners):
            x, y, z, core = target(dp // SIDE, dp % SIDE, zero // 2, zero % 2)
            pairs.append((dp * owners + zero, (x * SIDE + y) * owners + z * 2 + core))
    return pairs


def cube_pairs(mesh_sizes, dim):
    flip = (1, 3)[dim % 2]

    def target(x, y, z, core):
        along_x = (dim < 2) == (core == 0)
        return (x ^ flip, y, z, core) if along_x else (x, y ^ flip, z, core)

    return all_pairs(mesh_sizes, target)


def send(value, pairs):
    return lax.ppermute(value, ("dp", "zero"), pairs)


ORDERS = ((0, 1, 2, 3), (1, 0, 3, 2))


def cube_place(dp, core):
    x, y = gray(dp // SIDE), gray(dp % SIDE)
    return jnp.where(core == 0, x | (y << 2), y | (x << 2))


def cube_device(bits, core):
    first, second = gray(bits & 3), gray(bits >> 2)
    return jnp.where(core == 0, first * SIDE + second, second * SIDE + first)


def reduce_scatter(ordered, sizes):
    held = []
    for part, order in enumerate(ORDERS):
        rows = ordered[:, part * HALF : (part + 1) * HALF, :]
        rows = rows.reshape(2, 2, 2, 2, *rows.shape[1:])
        held.append((rows, [3, 2, 1, 0]))
    for step in range(4):
        sent, kept = [], []
        for (value, dims), order in zip(held, ORDERS):
            axis = dims.index(order[step])
            sent.append(lax.index_in_dim(value, 1, axis, keepdims=False).astype(BF16))
            kept.append(lax.index_in_dim(value, 0, axis, keepdims=False))
        received = [
            send(value, cube_pairs(sizes, order[step])) for value, order in zip(sent, ORDERS)
        ]
        held = [
            (mine.astype(F32) + other.astype(F32), [d for d in dims if d != order[step]])
            for mine, other, (_, dims), order in zip(kept, received, held, ORDERS)
        ]
    return [value for value, _ in held]


def assemble_kernel(place_ref, *refs):
    out_ref, sems = refs[-2], refs[-1]
    copies = []
    for part, order in enumerate(ORDERS):
        for late in range(2):
            source = refs[2 * part + late]
            for i in range(8):
                copies.append(
                    pltpu.make_async_copy(
                        source.at[i],
                        out_ref.at[place_ref[len(copies)], pl.ds(part * HALF, HALF)],
                        sems.at[len(copies)],
                    )
                )
                copies[-1].start()
    for copy in copies:
        copy.wait()


def all_gather(halves, sizes, me, core):
    held = [(half[None], []) for half in halves]
    for step in range(3, -1, -1):
        received = [
            send(value, cube_pairs(sizes, order[step]))
            for (value, _), order in zip(held, ORDERS)
        ]
        if step:
            held = [
                (jnp.concatenate([mine, other]), [order[step]] + dims)
                for (mine, dims), other, order in zip(held, received, ORDERS)
            ]
    places, pieces = [], []
    for (mine, dims), other, order in zip(held, received, ORDERS):
        pieces += [mine, other]
        for late in range(2):
            for i in range(8):
                relative = late << order[0]
                for at, dim in enumerate(dims):
                    relative |= ((i >> (2 - at)) & 1) << dim
                places.append(relative)
    places = cube_device(me ^ jnp.array(places, jnp.int32), core)
    width = halves[0].shape[-1]
    return pl.pallas_call(
        assemble_kernel,
        out_shape=jax.ShapeDtypeStruct((16, ROWS, width), BF16),
        grid_spec=pltpu.PrefetchScalarGridSpec(
            num_scalar_prefetch=1,
            grid=(),
            in_specs=[pl.BlockSpec(memory_space=pl.ANY)] * 4,
            out_specs=pl.BlockSpec(memory_space=pl.ANY),
            scratch_shapes=[pltpu.SemaphoreType.DMA((32,))],
        ),
        name="assemble",
    )(places, *pieces)


def split(value):
    high = value.astype(BF16)
    return high, (value - high.astype(F32)).astype(BF16)


def dot(a, b):
    return jnp.dot(a, b, preferred_element_type=F32)


def newton_schulz_kernel(mine_ref, other_ref, direction_ref, *out_refs):
    gram = mine_ref[...] + other_ref[...]
    row = lax.broadcasted_iota(jnp.int32, gram.shape, 0)
    column = lax.broadcasted_iota(jnp.int32, gram.shape, 1)
    total = jnp.sum(jnp.where(row == column, gram, 0.0))
    scale = 1.0 / (jnp.sqrt(jnp.full((1, 1), total, F32)) + tiny_value)
    gram = gram * scale * scale
    iterate = direction_ref[...].astype(F32)
    for repeat in range(ITERS):
        high, low = split(gram)
        polynomial = (coef_second * gram + coef_third * dot(high, high)).astype(BF16)
        x_high, x_low = split(iterate)
        product = dot(polynomial, x_high)
        if repeat:
            product += dot(polynomial, x_low)
        iterate = coef_first * iterate + product
        if repeat < ITERS - 1:
            left = coef_first * gram + (dot(polynomial, high) + dot(polynomial, low))
            high, low = split(left)
            gram = coef_first * left + (dot(high, polynomial) + dot(low, polynomial))
    factor = rms_factor * math.sqrt(max(ROWS, D))
    result = (iterate * (factor * scale)).astype(BF16)
    for part, ref in enumerate(out_refs):
        ref[...] = result[part * HALF : (part + 1) * HALF]


def newton_schulz(mine, other, direction):
    half = jax.ShapeDtypeStruct((HALF, direction.shape[1]), BF16)
    return pl.pallas_call(
        newton_schulz_kernel,
        out_shape=[half, half],
        compiler_params=pltpu.CompilerParams(vmem_limit_bytes=32 * 1024 * 1024),
        name="newton_schulz",
    )(mine, other, direction)


def gram_of(columns):
    return lax.dot_general(
        columns, columns, (((1,), (1,)), ((), ())), preferred_element_type=F32
    )


def per_device(sizes, gradients, momentum, bucket_slot):
    dp, zero = lax.axis_index("dp"), lax.axis_index("zero")
    replicas, owners = sizes
    core, chips = zero % 2, owners // 2
    me = cube_place(dp, core)
    slots = jnp.take(bucket_slot, cube_device(me ^ jnp.arange(16), core), mode="clip")
    ordered = jnp.take(gradients[0], slots, axis=0, mode="clip")
    with jax.named_scope("sum_over_replicas"):
        total = jnp.concatenate(reduce_scatter(ordered, sizes))
    average = total / replicas
    own = lax.dynamic_index_in_dim(momentum, dp, 0, keepdims=False).astype(F32)
    moment = (momentum_decay * own + average).astype(BF16)
    direction = (average + momentum_decay * moment.astype(F32)).astype(BF16)
    with jax.named_scope("moment_gather"):
        new_moment = lax.all_gather(moment, "dp", axis=0)
    swap = all_pairs(sizes, lambda x, y, z, c: (x, y, z, 1 - c))
    ring = all_pairs(sizes, lambda x, y, z, c: (x, y, (z + 1 - 2 * c) % chips, c))
    with jax.named_scope("gram_over_columns"):
        piece = jnp.concatenate([direction, send(direction, swap)], axis=1)
        gram = gram_of(direction)
        for step in range(1, chips // 2 + 1):
            if step == chips // 2:
                piece = piece[:, : direction.shape[1]]
            piece = send(piece, ring)
            gram = gram + gram_of(piece)
        other = send(gram, swap)
    halves = newton_schulz(gram, other, direction)
    with jax.named_scope("update_gather"):
        update = all_gather(halves, sizes, me, core)
    return (new_moment, update)


def solution(mesh):
    sizes = (mesh.shape["dp"], mesh.shape["zero"])
    return jax.shard_map(
        functools.partial(per_device, sizes),
        mesh=mesh,
        in_specs=(P("dp", None, None, "zero"), P(None, None, "zero"), P()),
        out_specs=(P(None, None, "zero"), P(None, None, "zero")),
        check_vma=False,
    )
```

```python
import functools
import math

import jax
import jax.numpy as jnp
from jax import lax
from jax.experimental import pallas as pl
from jax.experimental.pallas import tpu as pltpu
from jax.sharding import PartitionSpec as P

D = 4096
ROWS = 384
ITERS = 5

momentum_decay = 0.95
coef_first = 3.4445
coef_second = -4.775
coef_third = 2.0315
rms_factor = 0.2
tiny_value = 1e-07

BF16 = jnp.bfloat16
F32 = jnp.float32
SIDE = 4
HALF = ROWS // 2


def gray(position):
    return position ^ (position >> 1)


def all_pairs(mesh_sizes, target):
    replicas, owners = mesh_sizes
    pairs = []
    for dp in range(replicas):
        for zero in range(owners):
            x, y, z, core = target(dp // SIDE, dp % SIDE, zero // 2, zero % 2)
            pairs.append((dp * owners + zero, (x * SIDE + y) * owners + z * 2 + core))
    return pairs


def cube_pairs(mesh_sizes, dim):
    flip = (1, 3)[dim % 2]

    def target(x, y, z, core):
        along_x = (dim < 2) == (core == 0)
        return (x ^ flip, y, z, core) if along_x else (x, y ^ flip, z, core)

    return all_pairs(mesh_sizes, target)


def send(value, pairs):
    return lax.ppermute(value, ("dp", "zero"), pairs)


ORDERS = ((0, 1, 2, 3), (1, 0, 3, 2))


def cube_place(dp, core):
    x, y = gray(dp // SIDE), gray(dp % SIDE)
    return jnp.where(core == 0, x | (y << 2), y | (x << 2))


def cube_device(bits, core):
    first, second = gray(bits & 3), gray(bits >> 2)
    return jnp.where(core == 0, first * SIDE + second, second * SIDE + first)


def vmem(count):
    return [pl.BlockSpec(memory_space=pltpu.VMEM)] * count


def pack_kernel(slot_ref, gradients_ref, *out_refs):
    for part, out_ref in enumerate(out_refs):
        for i in range(8):
            slot = slot_ref[part * 8 + i]
            out_ref[i] = gradients_ref[slot, part * HALF : (part + 1) * HALF]


def pack(slots, gradients):
    half = jax.ShapeDtypeStruct((8, HALF, gradients.shape[-1]), BF16)
    return pl.pallas_call(
        pack_kernel,
        out_shape=[half, half],
        in_specs=[pl.BlockSpec(memory_space=pltpu.SMEM)] + vmem(1),
        out_specs=vmem(2),
        compiler_params=pltpu.CompilerParams(vmem_limit_bytes=16 * 1024 * 1024),
        cost_estimate=pl.CostEstimate(flops=0, bytes_accessed=6 << 20, transcendentals=0),
        name="pack",
    )(slots, gradients)


def relative_bits(dims):
    places = []
    for i in range(1 << len(dims)):
        place = 0
        for at, dim in enumerate(dims):
            place |= ((i >> (len(dims) - 1 - at)) & 1) << dim
        places.append(place)
    return places


def reduce_scatter(gradients, slots, sizes):
    sent_places, kept_places = [], []
    for order in ORDERS:
        rest = relative_bits(order[1:])
        sent_places += [place | 1 << order[0] for place in rest]
        kept_places += rest
    sent = pack(jnp.take(slots, jnp.array(sent_places), mode="clip"), gradients)
    received = [send(value, cube_pairs(sizes, order[0])) for value, order in zip(sent, ORDERS)]
    kept = pack(jnp.take(slots, jnp.array(kept_places), mode="clip"), gradients)
    for step in range(1, 4):
        half = kept[0].shape[0] // 2
        sent = [
            (mine[half:].astype(F32) + other[half:].astype(F32)).astype(BF16)
            for mine, other in zip(kept, received)
        ]
        kept = [
            mine[:half].astype(F32) + other[:half].astype(F32)
            for mine, other in zip(kept, received)
        ]
        received = [
            send(value, cube_pairs(sizes, order[step])) for value, order in zip(sent, ORDERS)
        ]
    return [(mine + other.astype(F32))[0] for mine, other in zip(kept, received)]


def assemble_kernel(place_ref, *refs):
    out_ref, sems = refs[-2], refs[-1]
    copies = []
    for part in range(2):
        for i in range(8):
            copies.append(
                pltpu.make_async_copy(
                    refs[part].at[i],
                    out_ref.at[place_ref[part * 8 + i], pl.ds(part * HALF, HALF)],
                    sems.at[part * 8 + i],
                )
            )
            copies[-1].start()
    for copy in copies:
        copy.wait()


def assemble(places, pieces, onto=None):
    width = pieces[0].shape[-1]
    anywhere = pl.BlockSpec(memory_space=pl.ANY)
    extra = [] if onto is None else [onto]
    return pl.pallas_call(
        assemble_kernel,
        out_shape=jax.ShapeDtypeStruct((16, ROWS, width), BF16),
        in_specs=[pl.BlockSpec(memory_space=pltpu.SMEM)] + vmem(2) + [anywhere] * len(extra),
        out_specs=anywhere,
        scratch_shapes=[pltpu.SemaphoreType.DMA((16,))],
        input_output_aliases={3: 0} if extra else {},
        compiler_params=pltpu.CompilerParams(vmem_limit_bytes=16 * 1024 * 1024),
        cost_estimate=pl.CostEstimate(flops=0, bytes_accessed=3 << 20, transcendentals=0),
        name="assemble",
    )(places, *pieces, *extra)


def all_gather(halves, sizes, me, core):
    held = [half[None] for half in halves]
    for step in range(3, -1, -1):
        received = [
            send(value, cube_pairs(sizes, order[step])) for value, order in zip(held, ORDERS)
        ]
        if step:
            held = [jnp.concatenate([mine, other]) for mine, other in zip(held, received)]
    near, far = [], []
    for order in ORDERS:
        rest = relative_bits(order[1:])
        near += rest
        far += [place | 1 << order[0] for place in rest]
    out = assemble(cube_device(me ^ jnp.array(near, jnp.int32), core), held)
    return assemble(cube_device(me ^ jnp.array(far, jnp.int32), core), received, out)


def split(value):
    high = value.astype(BF16)
    return high, (value - high.astype(F32)).astype(BF16)


def dot(a, b):
    return jnp.dot(a, b, preferred_element_type=F32)


def newton_schulz_kernel(mine_ref, other_ref, direction_ref, *out_refs):
    gram = mine_ref[...] + other_ref[...]
    row = lax.broadcasted_iota(jnp.int32, gram.shape, 0)
    column = lax.broadcasted_iota(jnp.int32, gram.shape, 1)
    total = jnp.sum(jnp.where(row == column, gram, 0.0))
    scale = 1.0 / (jnp.sqrt(jnp.full((1, 1), total, F32)) + tiny_value)
    gram = gram * scale * scale
    iterate = direction_ref[...].astype(F32)
    for repeat in range(ITERS):
        high, low = split(gram)
        polynomial = (coef_second * high.astype(F32) + coef_third * dot(high, high)).astype(BF16)
        x_high, x_low = split(iterate)
        product = dot(polynomial, x_high)
        if repeat:
            product += dot(polynomial, x_low)
        iterate = coef_first * iterate + product
        if repeat < ITERS - 1:
            left = coef_first * gram + (dot(polynomial, high) + dot(polynomial, low))
            high, low = split(left)
            gram = coef_first * left + (dot(high, polynomial) + dot(low, polynomial))
    factor = rms_factor * math.sqrt(max(ROWS, D))
    result = (iterate * (factor * scale)).astype(BF16)
    for part, ref in enumerate(out_refs):
        ref[...] = result[part * HALF : (part + 1) * HALF]


def newton_schulz(mine, other, direction):
    half = jax.ShapeDtypeStruct((HALF, direction.shape[1]), BF16)
    return pl.pallas_call(
        newton_schulz_kernel,
        out_shape=[half, half],
        in_specs=vmem(3),
        out_specs=vmem(2),
        compiler_params=pltpu.CompilerParams(vmem_limit_bytes=32 * 1024 * 1024),
        cost_estimate=pl.CostEstimate(flops=3 << 30, bytes_accessed=2 << 20, transcendentals=0),
        name="newton_schulz",
    )(mine, other, direction)


def gram_of(columns):
    return lax.dot_general(
        columns, columns, (((1,), (1,)), ((), ())), preferred_element_type=F32
    )


def per_device(sizes, gradients, momentum, bucket_slot):
    dp, zero = lax.axis_index("dp"), lax.axis_index("zero")
    replicas, owners = sizes
    core, chips = zero % 2, owners // 2
    me = cube_place(dp, core)
    slots = jnp.take(bucket_slot, cube_device(me ^ jnp.arange(16), core), mode="clip")
    with jax.named_scope("sum_over_replicas"):
        total = jnp.concatenate(reduce_scatter(gradients[0], slots, sizes))
    average = total / replicas
    own = lax.dynamic_index_in_dim(momentum, dp, 0, keepdims=False).astype(F32)
    moment = (momentum_decay * own + average).astype(BF16)
    direction = (average + momentum_decay * moment.astype(F32)).astype(BF16)
    swap = all_pairs(sizes, lambda x, y, z, c: (x, y, z, 1 - c))
    ring = all_pairs(sizes, lambda x, y, z, c: (x, y, (z + 1 - 2 * c) % chips, c))
    with jax.named_scope("gram_over_columns"):
        same, cross = direction, send(direction, swap)
        gram = gram_of(direction)
        for step in range(1, chips // 2 + 1):
            same = send(same, ring)
            gram = gram + gram_of(same)
            if step < chips // 2:
                cross = send(cross, ring)
                gram = gram + gram_of(cross)
        other = send(gram, swap)
    halves = newton_schulz(gram, other, direction)
    with jax.named_scope("moment_gather"):
        new_moment = all_gather([moment[:HALF], moment[HALF:]], sizes, me, core)
    with jax.named_scope("update_gather"):
        update = all_gather(halves, sizes, me, core)
    return (new_moment, update)


def solution(mesh):
    sizes = (mesh.shape["dp"], mesh.shape["zero"])
    return jax.shard_map(
        functools.partial(per_device, sizes),
        mesh=mesh,
        in_specs=(P("dp", None, None, "zero"), P(None, None, "zero"), P()),
        out_specs=(P(None, None, "zero"), P(None, None, "zero")),
        check_vma=False,
    )
```

```python
import functools
import math

import jax
import jax.numpy as jnp
from jax import lax
from jax.experimental import pallas as pl
from jax.experimental.pallas import tpu as pltpu
from jax.sharding import PartitionSpec as P

D = 4096
ROWS = 384
ITERS = 5

momentum_decay = 0.95
coef_first = 3.4445
coef_second = -4.775
coef_third = 2.0315
rms_factor = 0.2
tiny_value = 1e-07

BF16 = jnp.bfloat16
F32 = jnp.float32
SIDE = 4
HALF = ROWS // 2


def gray(position):
    return position ^ (position >> 1)


def all_pairs(mesh_sizes, target):
    replicas, owners = mesh_sizes
    pairs = []
    for dp in range(replicas):
        for zero in range(owners):
            x, y, z, core = target(dp // SIDE, dp % SIDE, zero // 2, zero % 2)
            pairs.append((dp * owners + zero, (x * SIDE + y) * owners + z * 2 + core))
    return pairs


def cube_pairs(mesh_sizes, *dims):
    flip = 0
    for dim in dims:
        flip ^= (1, 3)[dim % 2]

    def target(x, y, z, core):
        along_x = (dims[0] < 2) == (core == 0)
        return (x ^ flip, y, z, core) if along_x else (x, y ^ flip, z, core)

    return all_pairs(mesh_sizes, target)


def send(value, pairs):
    return lax.ppermute(value, ("dp", "zero"), pairs)


HEADS = ((0, 1), (1, 0))
TAIL = ((), (3,), (2,), (2, 3))


def cube_place(dp, core):
    x, y = gray(dp // SIDE), gray(dp % SIDE)
    return jnp.where(core == 0, x | (y << 2), y | (x << 2))


def cube_device(bits, core):
    first, second = gray(bits & 3), gray(bits >> 2)
    return jnp.where(core == 0, first * SIDE + second, second * SIDE + first)


def vmem(count):
    return [pl.BlockSpec(memory_space=pltpu.VMEM)] * count


def anywhere(count):
    return [pl.BlockSpec(memory_space=pl.ANY)] * count


def places_of(*dims):
    base = sum(1 << dim for dim in dims)
    return [base + sum(1 << dim for dim in tail) for tail in TAIL]


def kernel_device(relative):
    core = lax.rem(lax.axis_index("zero"), 2)
    return cube_device(cube_place(lax.axis_index("dp"), core) ^ relative, core)


def pack_kernel(places, slot_ref, gradients_ref, *out_refs):
    for part, (out_ref, own_places) in enumerate(zip(out_refs, places)):
        for i, place in enumerate(own_places):
            slot = slot_ref[kernel_device(place)]
            out_ref[i] = gradients_ref[slot, part * HALF : (part + 1) * HALF]


def pack(bucket_slot, gradients, places):
    width = gradients.shape[-1]
    count = sum(len(p) for p in places)
    return pl.pallas_call(
        functools.partial(pack_kernel, places),
        out_shape=[jax.ShapeDtypeStruct((len(p), HALF, width), BF16) for p in places],
        in_specs=[pl.BlockSpec(memory_space=pltpu.SMEM)] + vmem(1),
        out_specs=vmem(2),
        compiler_params=pltpu.CompilerParams(vmem_limit_bytes=16 * 1024 * 1024),
        cost_estimate=pl.CostEstimate(
            flops=0, bytes_accessed=2 * count * HALF * width * 2, transcendentals=0
        ),
        name="pack",
    )(bucket_slot, gradients)


def reduce_scatter(gradients, bucket_slot, sizes):
    away = [places_of(first) + places_of(first, second) for first, second in HEADS]
    kept = [places_of() + places_of(second) for _, second in HEADS]
    received = [
        send(v, cube_pairs(sizes, first))
        for v, (first, _) in zip(pack(bucket_slot, gradients, away), HEADS)
    ]
    kept = pack(bucket_slot, gradients, kept)
    sent = [(m[4:].astype(F32) + o[4:].astype(F32)).astype(BF16) for m, o in zip(kept, received)]
    kept = [m[:4].astype(F32) + o[:4].astype(F32) for m, o in zip(kept, received)]
    received = [send(v, cube_pairs(sizes, second)) for v, (_, second) in zip(sent, HEADS)]
    total = jnp.concatenate([m[0] + o[0].astype(F32) for m, o in zip(kept, received)])
    for i in range(1, 4):
        block = [(m[i] + o[i].astype(F32)).astype(BF16) for m, o in zip(kept, received)]
        total = total + send(jnp.concatenate(block), cube_pairs(sizes, *TAIL[i])).astype(F32)
    return total


def assemble_kernel(places, *refs):
    out_ref, sems = refs[-2], refs[-1]
    copies = []
    for ref, (part, own_places) in zip(refs, places):
        for i, place in enumerate(own_places):
            copies.append(
                pltpu.make_async_copy(
                    ref.at[i],
                    out_ref.at[kernel_device(place), pl.ds(part * HALF, HALF)],
                    sems.at[len(copies)],
                )
            )
            copies[-1].start()
    for copy in copies:
        copy.wait()


def assemble(pieces, places, onto=None, before=()):
    width = pieces[0].shape[-1]
    extra = ([] if onto is None else [onto]) + list(before)
    count = sum(len(p) for _, p in places)
    return pl.pallas_call(
        functools.partial(assemble_kernel, places),
        out_shape=jax.ShapeDtypeStruct((16, ROWS, width), BF16),
        in_specs=vmem(len(pieces)) + anywhere(len(extra)),
        out_specs=anywhere(1)[0],
        scratch_shapes=[pltpu.SemaphoreType.DMA((count,))],
        input_output_aliases={} if onto is None else {len(pieces): 0},
        compiler_params=pltpu.CompilerParams(vmem_limit_bytes=16 * 1024 * 1024),
        cost_estimate=pl.CostEstimate(
            flops=0, bytes_accessed=2 * count * HALF * width * 2, transcendentals=0
        ),
        name="assemble",
    )(*pieces, *extra)


def join_kernel(*refs):
    for part, out_ref in enumerate(refs[-2:]):
        for i in range(4):
            out_ref[i] = refs[i][part * HALF : (part + 1) * HALF]


def join(pieces, before):
    half = jax.ShapeDtypeStruct((4, HALF, pieces[0].shape[-1]), BF16)
    return pl.pallas_call(
        join_kernel,
        out_shape=[half, half],
        in_specs=vmem(4) + anywhere(len(before)),
        out_specs=vmem(2),
        compiler_params=pltpu.CompilerParams(vmem_limit_bytes=16 * 1024 * 1024),
        cost_estimate=pl.CostEstimate(flops=0, bytes_accessed=2 << 20, transcendentals=0),
        name="join",
    )(*pieces, *before)


def all_gather(value, sizes, before=()):
    pieces = [value] + [send(value, cube_pairs(sizes, *TAIL[i])) for i in range(1, 4)]
    four = join(pieces, before)
    side = [send(v, cube_pairs(sizes, second)) for v, (_, second) in zip(four, HEADS)]
    eight = [jnp.concatenate([m, o]) for m, o in zip(four, side)]
    received = [send(v, cube_pairs(sizes, first)) for v, (first, _) in zip(eight, HEADS)]
    return four, eight, received


def in_order(held, received, before=()):
    near = [(part, places_of() + places_of(second)) for part, (_, second) in enumerate(HEADS)]
    far = [
        (part, places_of(first) + places_of(first, second))
        for part, (first, second) in enumerate(HEADS)
    ]
    return assemble(received, far, assemble(held, near), before)


def split(value):
    high = value.astype(BF16)
    return high, (value - high.astype(F32)).astype(BF16)


def dot(a, b):
    return jnp.dot(a, b, preferred_element_type=F32)


def newton_schulz_kernel(mine_ref, other_ref, direction_ref, out_ref):
    gram = mine_ref[...] + other_ref[...]
    row = lax.broadcasted_iota(jnp.int32, gram.shape, 0)
    column = lax.broadcasted_iota(jnp.int32, gram.shape, 1)
    total = jnp.sum(jnp.where(row == column, gram, 0.0))
    scale = 1.0 / (jnp.sqrt(jnp.full((1, 1), total, F32)) + tiny_value)
    gram = gram * scale * scale
    iterate = direction_ref[...].astype(F32)
    for repeat in range(ITERS):
        high, low = split(gram)
        polynomial = (coef_second * high.astype(F32) + coef_third * dot(high, high)).astype(BF16)
        x_high, x_low = split(iterate)
        product = dot(polynomial, x_high)
        if repeat:
            product += dot(polynomial, x_low)
        iterate = coef_first * iterate + product
        if repeat < ITERS - 1:
            left = coef_first * gram + (dot(polynomial, high) + dot(polynomial, low))
            high, low = split(left)
            gram = coef_first * left + (dot(high, polynomial) + dot(low, polynomial))
    factor = rms_factor * math.sqrt(max(ROWS, D))
    out_ref[...] = (iterate * (factor * scale)).astype(BF16)


def newton_schulz(mine, other, direction):
    return pl.pallas_call(
        newton_schulz_kernel,
        out_shape=jax.ShapeDtypeStruct(direction.shape, BF16),
        in_specs=vmem(3),
        out_specs=vmem(1)[0],
        compiler_params=pltpu.CompilerParams(vmem_limit_bytes=32 * 1024 * 1024),
        cost_estimate=pl.CostEstimate(flops=7 << 30, bytes_accessed=2 << 20, transcendentals=0),
        name="newton_schulz",
    )(mine, other, direction)


def gram_kernel(added, *refs):
    total = None
    for ref in refs[:added]:
        block = ref[...]
        term = lax.dot_general(
            block, block, (((1,), (1,)), ((), ())), preferred_element_type=F32
        )
        total = term if total is None else total + term
    if added < len(refs) - 1 and refs[added].dtype == F32:
        total += refs[added][...]
    refs[-1][...] = total


def gram_of(columns, gram=None, before=()):
    extra = [] if gram is None else [gram]
    return pl.pallas_call(
        functools.partial(gram_kernel, len(columns)),
        out_shape=jax.ShapeDtypeStruct((ROWS, ROWS), F32),
        in_specs=vmem(len(columns) + len(extra)) + anywhere(len(before)),
        out_specs=vmem(1)[0],
        compiler_params=pltpu.CompilerParams(vmem_limit_bytes=16 * 1024 * 1024),
        cost_estimate=pl.CostEstimate(
            flops=len(columns) << 28, bytes_accessed=2 << 20, transcendentals=0
        ),
        name="gram",
    )(*columns, *extra, *before)


def per_device(sizes, gradients, momentum, bucket_slot):
    dp = lax.axis_index("dp")
    replicas, owners = sizes
    chips = owners // 2
    with jax.named_scope("sum_over_replicas"):
        total = reduce_scatter(gradients[0], bucket_slot, sizes)
    average = total / replicas
    own = lax.dynamic_index_in_dim(momentum, dp, 0, keepdims=False).astype(F32)
    moment = (momentum_decay * own + average).astype(BF16)
    direction = (average + momentum_decay * moment.astype(F32)).astype(BF16)
    swap = all_pairs(sizes, lambda x, y, z, c: (x, y, z, 1 - c))
    ring, skip = [
        all_pairs(sizes, lambda x, y, z, c, hops=hops: (x, y, (z + hops * (1 - 2 * c)) % chips, c))
        for hops in (1, 2)
    ]
    with jax.named_scope("moment_gather"):
        four, eight, rest = all_gather(moment, sizes)
    with jax.named_scope("gram_over_columns"):
        same, cross = send(direction, ring), send(send(direction, swap), ring)
        gram = gram_of([direction])
        gram = gram_of([same, cross], gram)
        same, cross = send(same, ring), send(cross, ring)
        gram = gram_of([same, cross], gram, four)
        same, cross, opposite = send(same, ring), send(cross, ring), send(same, skip)
        gram = gram_of([same, cross, opposite], gram, eight)
        other = send(gram, swap)
    update = newton_schulz(gram, other, direction)
    with jax.named_scope("update_gather"):
        _, *updates = all_gather(update, sizes, rest)
    new_moment = in_order(eight, rest)
    update = in_order(*updates, [new_moment])
    return (new_moment, update)


def solution(mesh):
    sizes = (mesh.shape["dp"], mesh.shape["zero"])
    return jax.shard_map(
        functools.partial(per_device, sizes),
        mesh=mesh,
        in_specs=(P("dp", None, None, "zero"), P(None, None, "zero"), P()),
        out_specs=(P(None, None, "zero"), P(None, None, "zero")),
        check_vma=False,
    )
```

```python
import functools
import math

import jax
import jax.numpy as jnp
from jax import lax
from jax.experimental import pallas as pl
from jax.experimental.pallas import tpu as pltpu
from jax.sharding import PartitionSpec as P

D = 4096
ROWS = 384
ITERS = 5

momentum_decay = 0.95
coef_first = 3.4445
coef_second = -4.775
coef_third = 2.0315
rms_factor = 0.2
tiny_value = 1e-07

BF16 = jnp.bfloat16
F32 = jnp.float32
SIDE = 4
HALF = ROWS // 2


def gray(position):
    return position ^ (position >> 1)


def all_pairs(mesh_sizes, target):
    replicas, owners = mesh_sizes
    pairs = []
    for dp in range(replicas):
        for zero in range(owners):
            x, y, z, core = target(dp // SIDE, dp % SIDE, zero // 2, zero % 2)
            pairs.append((dp * owners + zero, (x * SIDE + y) * owners + z * 2 + core))
    return pairs


def cube_pairs(mesh_sizes, *dims):
    flip = 0
    for dim in dims:
        flip ^= (1, 3)[dim % 2]

    def target(x, y, z, core):
        along_x = (dims[0] < 2) == (core == 0)
        return (x ^ flip, y, z, core) if along_x else (x, y ^ flip, z, core)

    return all_pairs(mesh_sizes, target)


def send(value, pairs):
    return lax.ppermute(value, ("dp", "zero"), pairs)


HEADS = ((0, 1), (1, 0))
TAIL = ((), (3,), (2,), (2, 3))


def cube_place(dp, core):
    x, y = gray(dp // SIDE), gray(dp % SIDE)
    return jnp.where(core == 0, x | (y << 2), y | (x << 2))


def cube_device(bits, core):
    first, second = gray(bits & 3), gray(bits >> 2)
    return jnp.where(core == 0, first * SIDE + second, second * SIDE + first)


def vmem(count):
    return [pl.BlockSpec(memory_space=pltpu.VMEM)] * count


def anywhere(count):
    return [pl.BlockSpec(memory_space=pl.ANY)] * count


def places_of(*dims):
    base = sum(1 << dim for dim in dims)
    return [base + sum(1 << dim for dim in tail) for tail in TAIL]


def kernel_device(relative):
    core = lax.rem(lax.axis_index("zero"), 2)
    return cube_device(cube_place(lax.axis_index("dp"), core) ^ relative, core)


def pack_kernel(places, slot_ref, gradients_ref, *out_refs):
    for part, (out_ref, own_places) in enumerate(zip(out_refs, places)):
        for i, place in enumerate(own_places):
            slot = slot_ref[kernel_device(place)]
            out_ref[i] = gradients_ref[slot, part * HALF : (part + 1) * HALF]


def pack(bucket_slot, gradients, places):
    width = gradients.shape[-1]
    count = sum(len(p) for p in places)
    return pl.pallas_call(
        functools.partial(pack_kernel, places),
        out_shape=[jax.ShapeDtypeStruct((len(p), HALF, width), BF16) for p in places],
        in_specs=[pl.BlockSpec(memory_space=pltpu.SMEM)] + vmem(1),
        out_specs=vmem(2),
        compiler_params=pltpu.CompilerParams(vmem_limit_bytes=16 * 1024 * 1024),
        cost_estimate=pl.CostEstimate(
            flops=0, bytes_accessed=2 * count * HALF * width * 2, transcendentals=0
        ),
        name="pack",
    )(bucket_slot, gradients)


def reduce_scatter(gradients, bucket_slot, sizes):
    away = [places_of(first) + places_of(first, second) for first, second in HEADS]
    kept = [places_of() + places_of(second) for _, second in HEADS]
    received = [
        send(v, cube_pairs(sizes, first))
        for v, (first, _) in zip(pack(bucket_slot, gradients, away), HEADS)
    ]
    kept = pack(bucket_slot, gradients, kept)
    sent = [(m[4:].astype(F32) + o[4:].astype(F32)).astype(BF16) for m, o in zip(kept, received)]
    kept = [m[:4].astype(F32) + o[:4].astype(F32) for m, o in zip(kept, received)]
    received = [send(v, cube_pairs(sizes, second)) for v, (_, second) in zip(sent, HEADS)]
    total = jnp.concatenate([m[0] + o[0].astype(F32) for m, o in zip(kept, received)])
    for i in range(1, 4):
        block = [(m[i] + o[i].astype(F32)).astype(BF16) for m, o in zip(kept, received)]
        total = total + send(jnp.concatenate(block), cube_pairs(sizes, *TAIL[i])).astype(F32)
    return total


def assemble_kernel(places, *refs):
    out_ref, sems = refs[-2], refs[-1]
    copies = []
    for ref, (part, own_places) in zip(refs, places):
        for i, place in enumerate(own_places):
            copies.append(
                pltpu.make_async_copy(
                    ref.at[i],
                    out_ref.at[kernel_device(place), pl.ds(part * HALF, HALF)],
                    sems.at[len(copies)],
                )
            )
            copies[-1].start()
    for copy in copies:
        copy.wait()


def assemble(pieces, places, onto=None, before=()):
    width = pieces[0].shape[-1]
    extra = ([] if onto is None else [onto]) + list(before)
    count = sum(len(p) for _, p in places)
    return pl.pallas_call(
        functools.partial(assemble_kernel, places),
        out_shape=jax.ShapeDtypeStruct((16, ROWS, width), BF16),
        in_specs=vmem(len(pieces)) + anywhere(len(extra)),
        out_specs=anywhere(1)[0],
        scratch_shapes=[pltpu.SemaphoreType.DMA((count,))],
        input_output_aliases={} if onto is None else {len(pieces): 0},
        compiler_params=pltpu.CompilerParams(vmem_limit_bytes=16 * 1024 * 1024),
        cost_estimate=pl.CostEstimate(
            flops=0, bytes_accessed=2 * count * HALF * width * 2, transcendentals=0
        ),
        name="assemble",
    )(*pieces, *extra)


def copy_rows_kernel(plan, *refs):
    outs = refs[len(refs) - 1 - max(out for out, *_ in plan) :]
    for out, i, piece, rows in plan:
        outs[out][i] = refs[piece][...] if rows is None else refs[piece][rows[0] : rows[1]]


def copy_rows(plan, pieces, counts, rows, before, flops=0):
    width = pieces[0].shape[-1]
    return pl.pallas_call(
        functools.partial(copy_rows_kernel, plan),
        out_shape=[jax.ShapeDtypeStruct((count, rows, width), BF16) for count in counts],
        in_specs=vmem(len(pieces)) + anywhere(len(before)),
        out_specs=vmem(len(counts)),
        compiler_params=pltpu.CompilerParams(vmem_limit_bytes=16 * 1024 * 1024),
        cost_estimate=pl.CostEstimate(
            flops=flops, bytes_accessed=4 * sum(counts) * rows * width, transcendentals=0
        ),
        name="copy_rows",
    )(*pieces, *before)


def join(pieces, before=()):
    plan = [
        (part, i, i, (part * HALF, (part + 1) * HALF)) for part in range(2) for i in range(4)
    ]
    return copy_rows(plan, pieces, [4, 4], HALF, before)


def append_kernel(first_ref, second_ref, *refs):
    out_ref = refs[-1]
    count = first_ref.shape[0]
    out_ref[:count] = first_ref[...]
    out_ref[count:] = second_ref[...]


def append(first, second, before):
    shape = (first.shape[0] + second.shape[0], *first.shape[1:])
    return pl.pallas_call(
        append_kernel,
        out_shape=jax.ShapeDtypeStruct(shape, first.dtype),
        in_specs=vmem(2) + anywhere(len(before)),
        out_specs=vmem(1)[0],
        compiler_params=pltpu.CompilerParams(vmem_limit_bytes=16 * 1024 * 1024),
        cost_estimate=pl.CostEstimate(flops=0, bytes_accessed=2 << 20, transcendentals=0),
        name="append",
    )(first, second, *before)


def all_gather(value, sizes, before=()):
    pieces = [value] + [send(value, cube_pairs(sizes, *TAIL[i])) for i in range(1, 4)]
    four = join(pieces)
    side = [send(v, cube_pairs(sizes, second)) for v, (_, second) in zip(four, HEADS)]
    eight = [append(m, o, before) for m, o in zip(four, side)]
    received = [send(v, cube_pairs(sizes, first)) for v, (first, _) in zip(eight, HEADS)]
    return four, eight, received


def in_order(held, received, before=()):
    near = [(part, places_of() + places_of(second)) for part, (_, second) in enumerate(HEADS)]
    far = [
        (part, places_of(first) + places_of(first, second))
        for part, (first, second) in enumerate(HEADS)
    ]
    out = assemble(held, near)
    out = assemble(received[:1], far[:1], out)
    return assemble(received[1:], far[1:], out, before)


def split(value):
    high = value.astype(BF16)
    return high, (value - high.astype(F32)).astype(BF16)


def dot(a, b):
    return jnp.dot(a, b, preferred_element_type=F32)


def newton_schulz_kernel(mine_ref, other_ref, direction_ref, out_ref):
    gram = mine_ref[...] + other_ref[...]
    row = lax.broadcasted_iota(jnp.int32, gram.shape, 0)
    column = lax.broadcasted_iota(jnp.int32, gram.shape, 1)
    total = jnp.sum(jnp.where(row == column, gram, 0.0))
    scale = 1.0 / (jnp.sqrt(jnp.full((1, 1), total, F32)) + tiny_value)
    gram = gram * scale * scale
    iterate = direction_ref[...]
    for repeat in range(ITERS):
        high, low = split(gram)
        polynomial = (coef_second * high.astype(F32) + coef_third * dot(high, high)).astype(BF16)
        product = dot(polynomial, iterate)
        iterate = coef_first * iterate.astype(F32) + product
        if repeat < ITERS - 1:
            iterate = iterate.astype(BF16)
            left = coef_first * gram + (dot(polynomial, high) + dot(polynomial, low))
            high, low = split(left)
            gram = coef_first * left + (dot(high, polynomial) + dot(low, polynomial))
    factor = rms_factor * math.sqrt(max(ROWS, D))
    out_ref[...] = (iterate * (factor * scale)).astype(BF16)


def newton_schulz(mine, other, direction):
    return pl.pallas_call(
        newton_schulz_kernel,
        out_shape=jax.ShapeDtypeStruct(direction.shape, BF16),
        in_specs=vmem(3),
        out_specs=vmem(1)[0],
        compiler_params=pltpu.CompilerParams(vmem_limit_bytes=32 * 1024 * 1024),
        cost_estimate=pl.CostEstimate(flops=7 << 30, bytes_accessed=2 << 20, transcendentals=0),
        name="newton_schulz",
    )(mine, other, direction)


def gram_kernel(added, *refs):
    total = None
    for ref in refs[:added]:
        block = ref[...]
        term = lax.dot_general(
            block, block, (((1,), (1,)), ((), ())), preferred_element_type=F32
        )
        total = term if total is None else total + term
    if added < len(refs) - 1 and refs[added].dtype == F32:
        total += refs[added][...]
    refs[-1][...] = total


def gram_of(columns, gram=None, before=()):
    extra = [] if gram is None else [gram]
    return pl.pallas_call(
        functools.partial(gram_kernel, len(columns)),
        out_shape=jax.ShapeDtypeStruct((ROWS, ROWS), F32),
        in_specs=vmem(len(columns) + len(extra)) + anywhere(len(before)),
        out_specs=vmem(1)[0],
        compiler_params=pltpu.CompilerParams(vmem_limit_bytes=16 * 1024 * 1024),
        cost_estimate=pl.CostEstimate(
            flops=len(columns) << 28, bytes_accessed=2 << 20, transcendentals=0
        ),
        name="gram",
    )(*columns, *extra, *before)


def per_device(sizes, gradients, momentum, bucket_slot):
    dp = lax.axis_index("dp")
    replicas, owners = sizes
    chips = owners // 2
    with jax.named_scope("sum_over_replicas"):
        total = reduce_scatter(gradients[0], bucket_slot, sizes)
    average = total / replicas
    own = lax.dynamic_index_in_dim(momentum, dp, 0, keepdims=False).astype(F32)
    moment = (momentum_decay * own + average).astype(BF16)
    direction = (average + momentum_decay * moment.astype(F32)).astype(BF16)
    swap = all_pairs(sizes, lambda x, y, z, c: (x, y, z, 1 - c))
    ring, skip = [
        all_pairs(sizes, lambda x, y, z, c, hops=hops: (x, y, (z + hops * (1 - 2 * c)) % chips, c))
        for hops in (1, 2)
    ]
    with jax.named_scope("gram_over_columns"):
        swapped = send(direction, swap)
        same, cross = send(direction, ring), send(swapped, ring)
        with jax.named_scope("moment_gather"):
            held = copy_rows([(0, 0, 0, None)], [moment], [1], ROWS, [swapped], 8 << 30)[0][0]
            four, eight, rest = all_gather(held, sizes)
        gram = gram_of([direction])
        gram = gram_of([same, cross], gram)
        same, cross = send(same, ring), send(cross, ring)
        gram = gram_of([same, cross], gram, four)
        same, cross, opposite = send(same, ring), send(cross, ring), send(same, skip)
        gram = gram_of([same, cross, opposite], gram, eight)
        other = send(gram, swap)
    update = newton_schulz(gram, other, direction)
    with jax.named_scope("update_gather"):
        _, *updates = all_gather(update, sizes, rest)
    new_moment = in_order(eight, rest)
    update = in_order(*updates, [new_moment])
    return (new_moment, update)


def solution(mesh):
    sizes = (mesh.shape["dp"], mesh.shape["zero"])
    return jax.shard_map(
        functools.partial(per_device, sizes),
        mesh=mesh,
        in_specs=(P("dp", None, None, "zero"), P(None, None, "zero"), P()),
        out_specs=(P(None, None, "zero"), P(None, None, "zero")),
        check_vma=False,
    )
```

```python
import functools
import math

import jax
import jax.numpy as jnp
from jax import lax
from jax.experimental import pallas as pl
from jax.experimental.pallas import tpu as pltpu
from jax.sharding import PartitionSpec as P

D = 4096
ROWS = 384
ITERS = 5

momentum_decay = 0.95
coef_first = 3.4445
coef_second = -4.775
coef_third = 2.0315
rms_factor = 0.2
tiny_value = 1e-07

BF16 = jnp.bfloat16
F32 = jnp.float32
SIDE = 4
HALF = ROWS // 2


def gray(position):
    return position ^ (position >> 1)


def all_pairs(mesh_sizes, target):
    replicas, owners = mesh_sizes
    pairs = []
    for dp in range(replicas):
        for zero in range(owners):
            x, y, z, core = target(dp // SIDE, dp % SIDE, zero // 2, zero % 2)
            pairs.append((dp * owners + zero, (x * SIDE + y) * owners + z * 2 + core))
    return pairs


def cube_pairs(mesh_sizes, *dims):
    flip = 0
    for dim in dims:
        flip ^= (1, 3)[dim % 2]

    def target(x, y, z, core):
        along_x = (dims[0] < 2) == (core == 0)
        return (x ^ flip, y, z, core) if along_x else (x, y ^ flip, z, core)

    return all_pairs(mesh_sizes, target)


def send(value, pairs):
    return lax.ppermute(value, ("dp", "zero"), pairs)


HEADS = ((0, 1), (1, 0))
TAIL = ((), (3,), (2,), (2, 3))


def cube_place(dp, core):
    x, y = gray(dp // SIDE), gray(dp % SIDE)
    return jnp.where(core == 0, x | (y << 2), y | (x << 2))


def cube_device(bits, core):
    first, second = gray(bits & 3), gray(bits >> 2)
    return jnp.where(core == 0, first * SIDE + second, second * SIDE + first)


def vmem(count):
    return [pl.BlockSpec(memory_space=pltpu.VMEM)] * count


def anywhere(count):
    return [pl.BlockSpec(memory_space=pl.ANY)] * count


def places_of(*dims):
    base = sum(1 << dim for dim in dims)
    return [base + sum(1 << dim for dim in tail) for tail in TAIL]


def kernel_device(relative):
    core = lax.rem(lax.axis_index("zero"), 2)
    return cube_device(cube_place(lax.axis_index("dp"), core) ^ relative, core)


def pack_kernel(places, slot_ref, gradients_ref, *out_refs):
    for part, (out_ref, own_places) in enumerate(zip(out_refs, places)):
        for i, place in enumerate(own_places):
            slot = slot_ref[kernel_device(place)]
            out_ref[i] = gradients_ref[slot, part * HALF : (part + 1) * HALF]


def pack(bucket_slot, gradients, places):
    width = gradients.shape[-1]
    count = sum(len(p) for p in places)
    return pl.pallas_call(
        functools.partial(pack_kernel, places),
        out_shape=[jax.ShapeDtypeStruct((len(p), HALF, width), BF16) for p in places],
        in_specs=[pl.BlockSpec(memory_space=pltpu.SMEM)] + vmem(1),
        out_specs=vmem(2),
        compiler_params=pltpu.CompilerParams(vmem_limit_bytes=16 * 1024 * 1024),
        cost_estimate=pl.CostEstimate(
            flops=0, bytes_accessed=2 * count * HALF * width * 2, transcendentals=0
        ),
        name="pack",
    )(bucket_slot, gradients)


def reduce_scatter(gradients, bucket_slot, sizes):
    away = [places_of(first) + places_of(first, second) for first, second in HEADS]
    kept = [places_of() + places_of(second) for _, second in HEADS]
    received = [
        send(v, cube_pairs(sizes, first))
        for v, (first, _) in zip(pack(bucket_slot, gradients, away), HEADS)
    ]
    kept = pack(bucket_slot, gradients, kept)
    sent = [(m[4:].astype(F32) + o[4:].astype(F32)).astype(BF16) for m, o in zip(kept, received)]
    kept = [m[:4].astype(F32) + o[:4].astype(F32) for m, o in zip(kept, received)]
    received = [send(v, cube_pairs(sizes, second)) for v, (_, second) in zip(sent, HEADS)]
    total = jnp.concatenate([m[0] + o[0].astype(F32) for m, o in zip(kept, received)])
    for i in range(1, 4):
        block = [(m[i] + o[i].astype(F32)).astype(BF16) for m, o in zip(kept, received)]
        total = total + send(jnp.concatenate(block), cube_pairs(sizes, *TAIL[i])).astype(F32)
    return total


def assemble_kernel(places, *refs):
    out_ref, sems = refs[-2], refs[-1]
    copies = []
    for ref, (part, own_places) in zip(refs, places):
        for i, place in enumerate(own_places):
            copies.append(
                pltpu.make_async_copy(
                    ref.at[i],
                    out_ref.at[kernel_device(place), pl.ds(part * HALF, HALF)],
                    sems.at[len(copies)],
                )
            )
            copies[-1].start()
    for copy in copies:
        copy.wait()


def assemble(pieces, places, onto=None, before=()):
    width = pieces[0].shape[-1]
    extra = ([] if onto is None else [onto]) + list(before)
    count = sum(len(p) for _, p in places)
    return pl.pallas_call(
        functools.partial(assemble_kernel, places),
        out_shape=jax.ShapeDtypeStruct((16, ROWS, width), BF16),
        in_specs=vmem(len(pieces)) + anywhere(len(extra)),
        out_specs=anywhere(1)[0],
        scratch_shapes=[pltpu.SemaphoreType.DMA((count,))],
        input_output_aliases={} if onto is None else {len(pieces): 0},
        compiler_params=pltpu.CompilerParams(vmem_limit_bytes=16 * 1024 * 1024),
        cost_estimate=pl.CostEstimate(
            flops=0, bytes_accessed=2 * count * HALF * width * 2, transcendentals=0
        ),
        name="assemble",
    )(*pieces, *extra)


def copy_rows_kernel(plan, *refs):
    outs = refs[len(refs) - 1 - max(out for out, *_ in plan) :]
    for out, i, piece, rows in plan:
        outs[out][i] = refs[piece][...] if rows is None else refs[piece][rows[0] : rows[1]]


def copy_rows(plan, pieces, counts, rows, before, flops=0):
    width = pieces[0].shape[-1]
    return pl.pallas_call(
        functools.partial(copy_rows_kernel, plan),
        out_shape=[jax.ShapeDtypeStruct((count, rows, width), BF16) for count in counts],
        in_specs=vmem(len(pieces)) + anywhere(len(before)),
        out_specs=vmem(len(counts)),
        compiler_params=pltpu.CompilerParams(vmem_limit_bytes=16 * 1024 * 1024),
        cost_estimate=pl.CostEstimate(
            flops=flops, bytes_accessed=4 * sum(counts) * rows * width, transcendentals=0
        ),
        name="copy_rows",
    )(*pieces, *before)


def join(pieces, before=()):
    plan = [
        (part, i, i, (part * HALF, (part + 1) * HALF)) for part in range(2) for i in range(4)
    ]
    return copy_rows(plan, pieces, [4, 4], HALF, before)


def append_kernel(first_ref, second_ref, *refs):
    out_ref = refs[-1]
    count = first_ref.shape[0]
    out_ref[:count] = first_ref[...]
    out_ref[count:] = second_ref[...]


def append(first, second, before):
    shape = (first.shape[0] + second.shape[0], *first.shape[1:])
    return pl.pallas_call(
        append_kernel,
        out_shape=jax.ShapeDtypeStruct(shape, first.dtype),
        in_specs=vmem(2) + anywhere(len(before)),
        out_specs=vmem(1)[0],
        compiler_params=pltpu.CompilerParams(vmem_limit_bytes=16 * 1024 * 1024),
        cost_estimate=pl.CostEstimate(flops=0, bytes_accessed=2 << 20, transcendentals=0),
        name="append",
    )(first, second, *before)


def all_gather(value, sizes, before=()):
    pieces = [value] + [send(value, cube_pairs(sizes, *TAIL[i])) for i in range(1, 4)]
    four = join(pieces)
    side = [send(v, cube_pairs(sizes, second)) for v, (_, second) in zip(four, HEADS)]
    eight = [append(m, o, before) for m, o in zip(four, side)]
    received = [send(v, cube_pairs(sizes, first)) for v, (first, _) in zip(eight, HEADS)]
    return four, eight, received


def in_order(held, received, before=()):
    near = [(part, places_of() + places_of(second)) for part, (_, second) in enumerate(HEADS)]
    far = [
        (part, places_of(first) + places_of(first, second))
        for part, (first, second) in enumerate(HEADS)
    ]
    out = assemble(held, near)
    out = assemble(received[:1], far[:1], out)
    return assemble(received[1:], far[1:], out, before)


def split(value):
    high = value.astype(BF16)
    return high, (value - high.astype(F32)).astype(BF16)


def dot(a, b):
    return jnp.dot(a, b, preferred_element_type=F32)


def newton_schulz_kernel(mine_ref, other_ref, direction_ref, out_ref):
    gram = mine_ref[...] + other_ref[...]
    row = lax.broadcasted_iota(jnp.int32, gram.shape, 0)
    column = lax.broadcasted_iota(jnp.int32, gram.shape, 1)
    total = jnp.sum(jnp.where(row == column, gram, 0.0))
    scale = 1.0 / (jnp.sqrt(jnp.full((1, 1), total, F32)) + tiny_value)
    gram = gram * scale * scale
    iterate = direction_ref[...]
    for repeat in range(ITERS):
        high, low = split(gram)
        polynomial = (coef_second * high.astype(F32) + coef_third * dot(high, high)).astype(BF16)
        product = dot(polynomial, iterate)
        iterate = coef_first * iterate.astype(F32) + product
        if repeat < ITERS - 1:
            iterate = iterate.astype(BF16)
            left = coef_first * gram + dot(
                jnp.concatenate([polynomial, polynomial], 1), jnp.concatenate([high, low], 0)
            )
            gram = coef_first * left + dot(
                jnp.concatenate(split(left), 1), jnp.concatenate([polynomial, polynomial], 0)
            )
    factor = rms_factor * math.sqrt(max(ROWS, D))
    out_ref[...] = (iterate * (factor * scale)).astype(BF16)


def newton_schulz(mine, other, direction):
    return pl.pallas_call(
        newton_schulz_kernel,
        out_shape=jax.ShapeDtypeStruct(direction.shape, BF16),
        in_specs=vmem(3),
        out_specs=vmem(1)[0],
        compiler_params=pltpu.CompilerParams(vmem_limit_bytes=32 * 1024 * 1024),
        cost_estimate=pl.CostEstimate(flops=7 << 30, bytes_accessed=2 << 20, transcendentals=0),
        name="newton_schulz",
    )(mine, other, direction)


def gram_kernel(added, *refs):
    total = None
    for ref in refs[:added]:
        block = ref[...]
        term = lax.dot_general(
            block, block, (((1,), (1,)), ((), ())), preferred_element_type=F32
        )
        total = term if total is None else total + term
    if added < len(refs) - 1 and refs[added].dtype == F32:
        total += refs[added][...]
    refs[-1][...] = total


def gram_of(columns, gram=None, before=()):
    extra = [] if gram is None else [gram]
    return pl.pallas_call(
        functools.partial(gram_kernel, len(columns)),
        out_shape=jax.ShapeDtypeStruct((ROWS, ROWS), F32),
        in_specs=vmem(len(columns) + len(extra)) + anywhere(len(before)),
        out_specs=vmem(1)[0],
        compiler_params=pltpu.CompilerParams(vmem_limit_bytes=16 * 1024 * 1024),
        cost_estimate=pl.CostEstimate(
            flops=len(columns) << 28, bytes_accessed=2 << 20, transcendentals=0
        ),
        name="gram",
    )(*columns, *extra, *before)


def per_device(sizes, gradients, momentum, bucket_slot):
    dp = lax.axis_index("dp")
    replicas, owners = sizes
    chips = owners // 2
    with jax.named_scope("sum_over_replicas"):
        total = reduce_scatter(gradients[0], bucket_slot, sizes)
    average = total / replicas
    own = lax.dynamic_index_in_dim(momentum, dp, 0, keepdims=False).astype(F32)
    moment = (momentum_decay * own + average).astype(BF16)
    direction = (average + momentum_decay * moment.astype(F32)).astype(BF16)
    swap = all_pairs(sizes, lambda x, y, z, c: (x, y, z, 1 - c))
    ring, skip = [
        all_pairs(sizes, lambda x, y, z, c, hops=hops: (x, y, (z + hops * (1 - 2 * c)) % chips, c))
        for hops in (1, 2)
    ]
    with jax.named_scope("gram_over_columns"):
        swapped = send(direction, swap)
        same, cross = send(direction, ring), send(swapped, ring)
        with jax.named_scope("moment_gather"):
            held = copy_rows([(0, 0, 0, None)], [moment], [1], ROWS, [swapped], 8 << 30)[0][0]
            four, eight, rest = all_gather(held, sizes)
        gram = gram_of([direction])
        gram = gram_of([same, cross], gram)
        same, cross = send(same, ring), send(cross, ring)
        gram = gram_of([same, cross], gram, four)
        same, cross, opposite = send(same, ring), send(cross, ring), send(same, skip)
        gram = gram_of([same, cross, opposite], gram, eight)
        other = send(gram, swap)
    update = newton_schulz(gram, other, direction)
    with jax.named_scope("update_gather"):
        _, *updates = all_gather(update, sizes, rest)
    new_moment = in_order(eight, rest)
    update = in_order(*updates, [new_moment])
    return (new_moment, update)


def solution(mesh):
    sizes = (mesh.shape["dp"], mesh.shape["zero"])
    return jax.shard_map(
        functools.partial(per_device, sizes),
        mesh=mesh,
        in_specs=(P("dp", None, None, "zero"), P(None, None, "zero"), P()),
        out_specs=(P(None, None, "zero"), P(None, None, "zero")),
        check_vma=False,
    )
```

```python
import functools
import math

import jax
import jax.numpy as jnp
from jax import lax
from jax.experimental import pallas as pl
from jax.experimental.pallas import tpu as pltpu
from jax.sharding import PartitionSpec as P

D = 4096
ROWS = 384
ITERS = 5

momentum_decay = 0.95
coef_first = 3.4445
coef_second = -4.775
coef_third = 2.0315
rms_factor = 0.2
tiny_value = 1e-07

BF16 = jnp.bfloat16
F32 = jnp.float32
SIDE = 4
HALF = ROWS // 2


def gray(position):
    return position ^ (position >> 1)


def all_pairs(mesh_sizes, target):
    replicas, owners = mesh_sizes
    pairs = []
    for dp in range(replicas):
        for zero in range(owners):
            x, y, z, core = target(dp // SIDE, dp % SIDE, zero // 2, zero % 2)
            pairs.append((dp * owners + zero, (x * SIDE + y) * owners + z * 2 + core))
    return pairs


def cube_pairs(mesh_sizes, *dims):
    flip = 0
    for dim in dims:
        flip ^= (1, 3)[dim % 2]

    def target(x, y, z, core):
        along_x = (dims[0] < 2) == (core == 0)
        return (x ^ flip, y, z, core) if along_x else (x, y ^ flip, z, core)

    return all_pairs(mesh_sizes, target)


def send(value, pairs):
    return lax.ppermute(value, ("dp", "zero"), pairs)


HEADS = ((0, 1), (1, 0))
TAIL = ((), (3,), (2,), (2, 3))


def cube_place(dp, core):
    x, y = gray(dp // SIDE), gray(dp % SIDE)
    return jnp.where(core == 0, x | (y << 2), y | (x << 2))


def cube_device(bits, core):
    first, second = gray(bits & 3), gray(bits >> 2)
    return jnp.where(core == 0, first * SIDE + second, second * SIDE + first)


def vmem(count):
    return [pl.BlockSpec(memory_space=pltpu.VMEM)] * count


def anywhere(count):
    return [pl.BlockSpec(memory_space=pl.ANY)] * count


def places_of(*dims):
    base = sum(1 << dim for dim in dims)
    return [base + sum(1 << dim for dim in tail) for tail in TAIL]


def kernel_device(relative):
    core = lax.rem(lax.axis_index("zero"), 2)
    return cube_device(cube_place(lax.axis_index("dp"), core) ^ relative, core)


def pack_kernel(places, slot_ref, gradients_ref, *refs):
    own = None
    if len(refs) > len(places):
        momentum_ref, *out_refs, own_ref, sem = refs
        own = pltpu.make_async_copy(momentum_ref.at[lax.axis_index("dp")], own_ref, sem)
        own.start()
    else:
        out_refs = refs
    for part, (out_ref, own_places) in enumerate(zip(out_refs, places)):
        for i, place in enumerate(own_places):
            slot = slot_ref[kernel_device(place)]
            out_ref[i] = gradients_ref[slot, part * HALF : (part + 1) * HALF]
    if own is not None:
        own.wait()


def pack(bucket_slot, gradients, places, momentum=()):
    width = gradients.shape[-1]
    count = sum(len(p) for p in places)
    return pl.pallas_call(
        functools.partial(pack_kernel, places),
        out_shape=[jax.ShapeDtypeStruct((len(p), HALF, width), BF16) for p in places]
        + [jax.ShapeDtypeStruct(m.shape[1:], m.dtype) for m in momentum],
        in_specs=[pl.BlockSpec(memory_space=pltpu.SMEM)] + vmem(1) + anywhere(len(momentum)),
        out_specs=vmem(2 + len(momentum)),
        scratch_shapes=[pltpu.SemaphoreType.DMA] * len(momentum),
        compiler_params=pltpu.CompilerParams(vmem_limit_bytes=16 * 1024 * 1024),
        cost_estimate=pl.CostEstimate(
            flops=0, bytes_accessed=2 * count * HALF * width * 2, transcendentals=0
        ),
        name="pack",
    )(bucket_slot, gradients, *momentum)


def reduce_scatter(gradients, momentum, bucket_slot, sizes):
    away = [places_of(first) + places_of(first, second) for first, second in HEADS]
    kept = [places_of() + places_of(second) for _, second in HEADS]
    received = [
        send(v, cube_pairs(sizes, first))
        for v, (first, _) in zip(pack(bucket_slot, gradients, away), HEADS)
    ]
    *kept, own = pack(bucket_slot, gradients, kept, [momentum])
    sent = [(m[4:].astype(F32) + o[4:].astype(F32)).astype(BF16) for m, o in zip(kept, received)]
    kept = [m[:4].astype(F32) + o[:4].astype(F32) for m, o in zip(kept, received)]
    received = [send(v, cube_pairs(sizes, second)) for v, (_, second) in zip(sent, HEADS)]
    total = jnp.concatenate([m[0] + o[0].astype(F32) for m, o in zip(kept, received)])
    for i in range(1, 4):
        block = [(m[i] + o[i].astype(F32)).astype(BF16) for m, o in zip(kept, received)]
        total = total + send(jnp.concatenate(block), cube_pairs(sizes, *TAIL[i])).astype(F32)
    return total, own


def assemble_kernel(places, *refs):
    out_ref, sems = refs[-2], refs[-1]
    copies = []
    for ref, (part, own_places) in zip(refs, places):
        for i, place in enumerate(own_places):
            copies.append(
                pltpu.make_async_copy(
                    ref.at[i],
                    out_ref.at[kernel_device(place), pl.ds(part * HALF, HALF)],
                    sems.at[len(copies)],
                )
            )
            copies[-1].start()
    for copy in copies:
        copy.wait()


def assemble(pieces, places, onto=None, before=()):
    width = pieces[0].shape[-1]
    extra = ([] if onto is None else [onto]) + list(before)
    count = sum(len(p) for _, p in places)
    return pl.pallas_call(
        functools.partial(assemble_kernel, places),
        out_shape=jax.ShapeDtypeStruct((16, ROWS, width), BF16),
        in_specs=vmem(len(pieces)) + anywhere(len(extra)),
        out_specs=anywhere(1)[0],
        scratch_shapes=[pltpu.SemaphoreType.DMA((count,))],
        input_output_aliases={} if onto is None else {len(pieces): 0},
        compiler_params=pltpu.CompilerParams(vmem_limit_bytes=16 * 1024 * 1024),
        cost_estimate=pl.CostEstimate(
            flops=0, bytes_accessed=2 * count * HALF * width * 2, transcendentals=0
        ),
        name="assemble",
    )(*pieces, *extra)


def copy_rows_kernel(plan, *refs):
    outs = refs[len(refs) - 1 - max(out for out, *_ in plan) :]
    for out, i, piece, rows in plan:
        outs[out][i] = refs[piece][...] if rows is None else refs[piece][rows[0] : rows[1]]


def copy_rows(plan, pieces, counts, rows, before, flops=0):
    width = pieces[0].shape[-1]
    return pl.pallas_call(
        functools.partial(copy_rows_kernel, plan),
        out_shape=[jax.ShapeDtypeStruct((count, rows, width), BF16) for count in counts],
        in_specs=vmem(len(pieces)) + anywhere(len(before)),
        out_specs=vmem(len(counts)),
        compiler_params=pltpu.CompilerParams(vmem_limit_bytes=16 * 1024 * 1024),
        cost_estimate=pl.CostEstimate(
            flops=flops, bytes_accessed=4 * sum(counts) * rows * width, transcendentals=0
        ),
        name="copy_rows",
    )(*pieces, *before)


def join(pieces, before=()):
    plan = [
        (part, i, i, (part * HALF, (part + 1) * HALF)) for part in range(2) for i in range(4)
    ]
    return copy_rows(plan, pieces, [4, 4], HALF, before)


def append_kernel(first_ref, second_ref, *refs):
    out_ref = refs[-1]
    count = first_ref.shape[0]
    out_ref[:count] = first_ref[...]
    out_ref[count:] = second_ref[...]


def append(first, second, before):
    shape = (first.shape[0] + second.shape[0], *first.shape[1:])
    return pl.pallas_call(
        append_kernel,
        out_shape=jax.ShapeDtypeStruct(shape, first.dtype),
        in_specs=vmem(2) + anywhere(len(before)),
        out_specs=vmem(1)[0],
        compiler_params=pltpu.CompilerParams(vmem_limit_bytes=16 * 1024 * 1024),
        cost_estimate=pl.CostEstimate(flops=0, bytes_accessed=2 << 20, transcendentals=0),
        name="append",
    )(first, second, *before)


def all_gather(value, sizes, before=()):
    pieces = [value] + [send(value, cube_pairs(sizes, *TAIL[i])) for i in range(1, 4)]
    four = join(pieces)
    side = [send(v, cube_pairs(sizes, second)) for v, (_, second) in zip(four, HEADS)]
    eight = [append(m, o, before) for m, o in zip(four, side)]
    received = [send(v, cube_pairs(sizes, first)) for v, (first, _) in zip(eight, HEADS)]
    return four, eight, received


def in_order(held, received, before=()):
    near = [(part, places_of() + places_of(second)) for part, (_, second) in enumerate(HEADS)]
    far = [
        (part, places_of(first) + places_of(first, second))
        for part, (first, second) in enumerate(HEADS)
    ]
    out = assemble(held, near)
    out = assemble(received[:1], far[:1], out)
    return assemble(received[1:], far[1:], out, before)


def split(value):
    high = value.astype(BF16)
    return high, (value - high.astype(F32)).astype(BF16)


def dot(a, b):
    return jnp.dot(a, b, preferred_element_type=F32)


def newton_schulz_kernel(mine_ref, other_ref, direction_ref, out_ref):
    gram = mine_ref[...] + other_ref[...]
    row = lax.broadcasted_iota(jnp.int32, gram.shape, 0)
    column = lax.broadcasted_iota(jnp.int32, gram.shape, 1)
    total = jnp.sum(jnp.where(row == column, gram, 0.0))
    scale = 1.0 / (jnp.sqrt(jnp.full((1, 1), total, F32)) + tiny_value)
    gram = gram * scale * scale
    iterate = direction_ref[...]
    for repeat in range(ITERS):
        high, low = split(gram)
        polynomial = (coef_second * high.astype(F32) + coef_third * dot(high, high)).astype(BF16)
        product = dot(polynomial, iterate)
        iterate = coef_first * iterate.astype(F32) + product
        if repeat < ITERS - 1:
            iterate = iterate.astype(BF16)
            left = coef_first * gram + dot(
                jnp.concatenate([polynomial, polynomial], 1), jnp.concatenate([high, low], 0)
            )
            gram = coef_first * left + dot(
                jnp.concatenate(split(left), 1), jnp.concatenate([polynomial, polynomial], 0)
            )
    factor = rms_factor * math.sqrt(max(ROWS, D))
    out_ref[...] = (iterate * (factor * scale)).astype(BF16)


def newton_schulz(mine, other, direction):
    return pl.pallas_call(
        newton_schulz_kernel,
        out_shape=jax.ShapeDtypeStruct(direction.shape, BF16),
        in_specs=vmem(3),
        out_specs=vmem(1)[0],
        compiler_params=pltpu.CompilerParams(vmem_limit_bytes=32 * 1024 * 1024),
        cost_estimate=pl.CostEstimate(flops=7 << 30, bytes_accessed=2 << 20, transcendentals=0),
        name="newton_schulz",
    )(mine, other, direction)


def gram_kernel(added, *refs):
    total = None
    for ref in refs[:added]:
        block = ref[...]
        term = lax.dot_general(
            block, block, (((1,), (1,)), ((), ())), preferred_element_type=F32
        )
        total = term if total is None else total + term
    if added < len(refs) - 1 and refs[added].dtype == F32:
        total += refs[added][...]
    refs[-1][...] = total


def gram_of(columns, gram=None, before=()):
    extra = [] if gram is None else [gram]
    return pl.pallas_call(
        functools.partial(gram_kernel, len(columns)),
        out_shape=jax.ShapeDtypeStruct((ROWS, ROWS), F32),
        in_specs=vmem(len(columns) + len(extra)) + anywhere(len(before)),
        out_specs=vmem(1)[0],
        compiler_params=pltpu.CompilerParams(vmem_limit_bytes=16 * 1024 * 1024),
        cost_estimate=pl.CostEstimate(
            flops=len(columns) << 28, bytes_accessed=2 << 20, transcendentals=0
        ),
        name="gram",
    )(*columns, *extra, *before)


def per_device(sizes, gradients, momentum, bucket_slot):
    replicas, owners = sizes
    chips = owners // 2
    with jax.named_scope("sum_over_replicas"):
        total, own = reduce_scatter(gradients[0], momentum, bucket_slot, sizes)
    average = total / replicas
    own = own.astype(F32)
    moment = (momentum_decay * own + average).astype(BF16)
    direction = (average + momentum_decay * moment.astype(F32)).astype(BF16)
    swap = all_pairs(sizes, lambda x, y, z, c: (x, y, z, 1 - c))
    ring, skip = [
        all_pairs(sizes, lambda x, y, z, c, hops=hops: (x, y, (z + hops * (1 - 2 * c)) % chips, c))
        for hops in (1, 2)
    ]
    with jax.named_scope("gram_over_columns"):
        swapped = send(direction, swap)
        same, cross = send(direction, ring), send(swapped, ring)
        with jax.named_scope("moment_gather"):
            held = copy_rows([(0, 0, 0, None)], [moment], [1], ROWS, [swapped], 8 << 30)[0][0]
            four, eight, rest = all_gather(held, sizes)
        gram = gram_of([direction])
        gram = gram_of([same, cross], gram)
        same, cross = send(same, ring), send(cross, ring)
        gram = gram_of([same, cross], gram, four)
        same, cross, opposite = send(same, ring), send(cross, ring), send(same, skip)
        gram = gram_of([same, cross, opposite], gram, eight)
        other = send(gram, swap)
    update = newton_schulz(gram, other, direction)
    with jax.named_scope("update_gather"):
        _, *updates = all_gather(update, sizes, rest)
    new_moment = in_order(eight, rest)
    update = in_order(*updates, [new_moment])
    return (new_moment, update)


def solution(mesh):
    sizes = (mesh.shape["dp"], mesh.shape["zero"])
    return jax.shard_map(
        functools.partial(per_device, sizes),
        mesh=mesh,
        in_specs=(P("dp", None, None, "zero"), P(None, None, "zero"), P()),
        out_specs=(P(None, None, "zero"), P(None, None, "zero")),
        check_vma=False,
    )
```

```python
import functools
import math

import jax
import jax.numpy as jnp
from jax import lax
from jax.experimental import pallas as pl
from jax.experimental.pallas import tpu as pltpu
from jax.sharding import PartitionSpec as P

D = 4096
ROWS = 384
ITERS = 5

momentum_decay = 0.95
coef_first = 3.4445
coef_second = -4.775
coef_third = 2.0315
rms_factor = 0.2
tiny_value = 1e-07

BF16 = jnp.bfloat16
F32 = jnp.float32
SIDE = 4
HALF = ROWS // 2


def gray(position):
    return position ^ (position >> 1)


def all_pairs(mesh_sizes, target):
    replicas, owners = mesh_sizes
    pairs = []
    for dp in range(replicas):
        for zero in range(owners):
            x, y, z, core = target(dp // SIDE, dp % SIDE, zero // 2, zero % 2)
            pairs.append((dp * owners + zero, (x * SIDE + y) * owners + z * 2 + core))
    return pairs


def cube_pairs(mesh_sizes, *dims):
    flip = 0
    for dim in dims:
        flip ^= (1, 3)[dim % 2]

    def target(x, y, z, core):
        along_x = (dims[0] < 2) == (core == 0)
        return (x ^ flip, y, z, core) if along_x else (x, y ^ flip, z, core)

    return all_pairs(mesh_sizes, target)


def send(value, pairs):
    return lax.ppermute(value, ("dp", "zero"), pairs)


HEADS = ((0, 1), (1, 0))
TAIL = ((), (3,), (2,), (2, 3))


def cube_place(dp, core):
    x, y = gray(dp // SIDE), gray(dp % SIDE)
    return jnp.where(core == 0, x | (y << 2), y | (x << 2))


def cube_device(bits, core):
    first, second = gray(bits & 3), gray(bits >> 2)
    return jnp.where(core == 0, first * SIDE + second, second * SIDE + first)


def vmem(count):
    return [pl.BlockSpec(memory_space=pltpu.VMEM)] * count


def anywhere(count):
    return [pl.BlockSpec(memory_space=pl.ANY)] * count


def places_of(*dims):
    base = sum(1 << dim for dim in dims)
    return [base + sum(1 << dim for dim in tail) for tail in TAIL]


def kernel_device(relative):
    core = lax.rem(lax.axis_index("zero"), 2)
    return cube_device(cube_place(lax.axis_index("dp"), core) ^ relative, core)


def pack_kernel(places, slot_ref, gradients_ref, *refs):
    own = None
    if len(refs) > len(places):
        momentum_ref, *out_refs, own_ref, sem = refs
        own = pltpu.make_async_copy(momentum_ref.at[lax.axis_index("dp")], own_ref, sem)
        own.start()
    else:
        out_refs = refs
    for part, (out_ref, own_places) in enumerate(zip(out_refs, places)):
        for i, place in enumerate(own_places):
            slot = slot_ref[kernel_device(place)]
            out_ref[i] = gradients_ref[slot, part * HALF : (part + 1) * HALF]
    if own is not None:
        own.wait()


def pack(bucket_slot, gradients, places, momentum=()):
    width = gradients.shape[-1]
    count = sum(len(p) for p in places)
    return pl.pallas_call(
        functools.partial(pack_kernel, places),
        out_shape=[jax.ShapeDtypeStruct((len(p), HALF, width), BF16) for p in places]
        + [jax.ShapeDtypeStruct(m.shape[1:], m.dtype) for m in momentum],
        in_specs=[pl.BlockSpec(memory_space=pltpu.SMEM)] + vmem(1) + anywhere(len(momentum)),
        out_specs=vmem(2 + len(momentum)),
        scratch_shapes=[pltpu.SemaphoreType.DMA] * len(momentum),
        compiler_params=pltpu.CompilerParams(vmem_limit_bytes=16 * 1024 * 1024),
        cost_estimate=pl.CostEstimate(
            flops=0, bytes_accessed=2 * count * HALF * width * 2, transcendentals=0
        ),
        name="pack",
    )(bucket_slot, gradients, *momentum)


def reduce_scatter(gradients, momentum, bucket_slot, sizes):
    away = [places_of(first) + places_of(first, second) for first, second in HEADS]
    kept = [places_of() + places_of(second) for _, second in HEADS]
    received = [
        send(v, cube_pairs(sizes, first))
        for v, (first, _) in zip(pack(bucket_slot, gradients, away), HEADS)
    ]
    *kept, own = pack(bucket_slot, gradients, kept, [momentum])
    sent = [(m[4:].astype(F32) + o[4:].astype(F32)).astype(BF16) for m, o in zip(kept, received)]
    kept = [m[:4].astype(F32) + o[:4].astype(F32) for m, o in zip(kept, received)]
    received = [send(v, cube_pairs(sizes, second)) for v, (_, second) in zip(sent, HEADS)]
    total = jnp.concatenate([m[0] + o[0].astype(F32) for m, o in zip(kept, received)])
    for i in range(1, 4):
        block = [(m[i] + o[i].astype(F32)).astype(BF16) for m, o in zip(kept, received)]
        total = total + send(jnp.concatenate(block), cube_pairs(sizes, *TAIL[i])).astype(F32)
    return total, own


def assemble_kernel(places, *refs):
    out_ref, sems = refs[-2], refs[-1]
    copies = []
    for ref, (part, own_places) in zip(refs, places):
        for i, place in enumerate(own_places):
            copies.append(
                pltpu.make_async_copy(
                    ref.at[i],
                    out_ref.at[kernel_device(place), pl.ds(part * HALF, HALF)],
                    sems.at[len(copies)],
                )
            )
            copies[-1].start()
    for copy in copies:
        copy.wait()


def assemble(pieces, places, onto=None, before=()):
    width = pieces[0].shape[-1]
    extra = ([] if onto is None else [onto]) + list(before)
    count = sum(len(p) for _, p in places)
    return pl.pallas_call(
        functools.partial(assemble_kernel, places),
        out_shape=jax.ShapeDtypeStruct((16, ROWS, width), BF16),
        in_specs=vmem(len(pieces)) + anywhere(len(extra)),
        out_specs=anywhere(1)[0],
        scratch_shapes=[pltpu.SemaphoreType.DMA((count,))],
        input_output_aliases={} if onto is None else {len(pieces): 0},
        compiler_params=pltpu.CompilerParams(vmem_limit_bytes=16 * 1024 * 1024),
        cost_estimate=pl.CostEstimate(
            flops=0, bytes_accessed=2 * count * HALF * width * 2, transcendentals=0
        ),
        name="assemble",
    )(*pieces, *extra)


def copy_rows_kernel(plan, *refs):
    outs = refs[len(refs) - 1 - max(out for out, *_ in plan) :]
    for out, i, piece, rows in plan:
        outs[out][i] = refs[piece][...] if rows is None else refs[piece][rows[0] : rows[1]]


def copy_rows(plan, pieces, counts, rows, before, flops=0):
    width = pieces[0].shape[-1]
    return pl.pallas_call(
        functools.partial(copy_rows_kernel, plan),
        out_shape=[jax.ShapeDtypeStruct((count, rows, width), BF16) for count in counts],
        in_specs=vmem(len(pieces)) + anywhere(len(before)),
        out_specs=vmem(len(counts)),
        compiler_params=pltpu.CompilerParams(vmem_limit_bytes=16 * 1024 * 1024),
        cost_estimate=pl.CostEstimate(
            flops=flops, bytes_accessed=4 * sum(counts) * rows * width, transcendentals=0
        ),
        name="copy_rows",
    )(*pieces, *before)


def join(pieces, before=()):
    plan = [
        (part, i, i, (part * HALF, (part + 1) * HALF)) for part in range(2) for i in range(4)
    ]
    return copy_rows(plan, pieces, [4, 4], HALF, before)


def append_kernel(first_ref, second_ref, *refs):
    out_ref = refs[-1]
    count = first_ref.shape[0]
    out_ref[:count] = first_ref[...]
    out_ref[count:] = second_ref[...]


def append(first, second, before):
    shape = (first.shape[0] + second.shape[0], *first.shape[1:])
    return pl.pallas_call(
        append_kernel,
        out_shape=jax.ShapeDtypeStruct(shape, first.dtype),
        in_specs=vmem(2) + anywhere(len(before)),
        out_specs=vmem(1)[0],
        compiler_params=pltpu.CompilerParams(vmem_limit_bytes=16 * 1024 * 1024),
        cost_estimate=pl.CostEstimate(flops=0, bytes_accessed=2 << 20, transcendentals=0),
        name="append",
    )(first, second, *before)


def all_gather(value, sizes, before=()):
    pieces = [value] + [send(value, cube_pairs(sizes, *TAIL[i])) for i in range(1, 4)]
    four = join(pieces)
    side = [send(v, cube_pairs(sizes, second)) for v, (_, second) in zip(four, HEADS)]
    eight = [append(m, o, before) for m, o in zip(four, side)]
    received = [send(v, cube_pairs(sizes, first)) for v, (first, _) in zip(eight, HEADS)]
    return four, eight, received


def in_order(held, received, before=()):
    near = [(part, places_of() + places_of(second)) for part, (_, second) in enumerate(HEADS)]
    far = [
        (part, places_of(first) + places_of(first, second))
        for part, (first, second) in enumerate(HEADS)
    ]
    out = assemble(held, near)
    out = assemble(received[:1], far[:1], out)
    return assemble(received[1:], far[1:], out, before)


def split(value):
    high = value.astype(BF16)
    return high, (value - high.astype(F32)).astype(BF16)


def dot(a, b):
    return jnp.dot(a, b, preferred_element_type=F32)


def newton_schulz_kernel(mine_ref, other_ref, direction_ref, out_ref):
    gram = mine_ref[...] + other_ref[...]
    row = lax.broadcasted_iota(jnp.int32, gram.shape, 0)
    column = lax.broadcasted_iota(jnp.int32, gram.shape, 1)
    total = jnp.sum(jnp.where(row == column, gram, 0.0))
    scale = 1.0 / (jnp.sqrt(jnp.full((1, 1), total, F32)) + tiny_value)
    gram = gram * scale * scale
    iterate = direction_ref[...]
    for repeat in range(ITERS):
        high, low = split(gram)
        polynomial = (coef_second * high.astype(F32) + coef_third * dot(high, high)).astype(BF16)
        product = dot(polynomial, iterate)
        iterate = coef_first * iterate.astype(F32) + product
        if repeat < ITERS - 1:
            iterate = iterate.astype(BF16)
            left = coef_first * gram + dot(
                jnp.concatenate([polynomial, polynomial], 1), jnp.concatenate([high, low], 0)
            )
            gram = coef_first * left + dot(
                jnp.concatenate(split(left), 1), jnp.concatenate([polynomial, polynomial], 0)
            )
    factor = rms_factor * math.sqrt(max(ROWS, D))
    out_ref[...] = (iterate * (factor * scale)).astype(BF16)


def newton_schulz(mine, other, direction):
    return pl.pallas_call(
        newton_schulz_kernel,
        out_shape=jax.ShapeDtypeStruct(direction.shape, BF16),
        in_specs=vmem(3),
        out_specs=vmem(1)[0],
        compiler_params=pltpu.CompilerParams(vmem_limit_bytes=32 * 1024 * 1024),
        cost_estimate=pl.CostEstimate(flops=7 << 30, bytes_accessed=2 << 20, transcendentals=0),
        name="newton_schulz",
    )(mine, other, direction)


def gram_kernel(added, *refs):
    total = None
    for ref in refs[:added]:
        block = ref[...]
        term = lax.dot_general(
            block, block, (((1,), (1,)), ((), ())), preferred_element_type=F32
        )
        total = term if total is None else total + term
    if added < len(refs) - 1 and refs[added].dtype == F32:
        total += refs[added][...]
    refs[-1][...] = total


def gram_of(columns, gram=None, before=()):
    extra = [] if gram is None else [gram]
    return pl.pallas_call(
        functools.partial(gram_kernel, len(columns)),
        out_shape=jax.ShapeDtypeStruct((ROWS, ROWS), F32),
        in_specs=vmem(len(columns) + len(extra)) + anywhere(len(before)),
        out_specs=vmem(1)[0],
        compiler_params=pltpu.CompilerParams(vmem_limit_bytes=16 * 1024 * 1024),
        cost_estimate=pl.CostEstimate(
            flops=len(columns) << 28, bytes_accessed=2 << 20, transcendentals=0
        ),
        name="gram",
    )(*columns, *extra, *before)


def per_device(sizes, gradients, momentum, bucket_slot):
    replicas, owners = sizes
    chips = owners // 2
    with jax.named_scope("sum_over_replicas"):
        total, own = reduce_scatter(gradients[0], momentum, bucket_slot, sizes)
    average = total / replicas
    own = own.astype(F32)
    moment = (momentum_decay * own + average).astype(BF16)
    direction = (average + momentum_decay * moment.astype(F32)).astype(BF16)
    swap = all_pairs(sizes, lambda x, y, z, c: (x, y, z, 1 - c))
    ring, skip = [
        all_pairs(sizes, lambda x, y, z, c, hops=hops: (x, y, (z + hops * (1 - 2 * c)) % chips, c))
        for hops in (1, 2)
    ]
    with jax.named_scope("gram_over_columns"):
        swapped = send(direction, swap)
        same, cross = send(direction, ring), send(swapped, ring)
        with jax.named_scope("moment_gather"):
            held = copy_rows([(0, 0, 0, None)], [moment], [1], ROWS, [swapped], 8 << 30)[0][0]
            four, eight, rest = all_gather(held, sizes)
        gram = gram_of([direction])
        gram = gram_of([same, cross], gram)
        same, cross = send(same, ring), send(cross, ring)
        gram = gram_of([same, cross], gram, four)
        same, cross, opposite = send(same, ring), send(cross, ring), send(same, skip)
        gram = gram_of([same, opposite], gram, eight)
        gram = gram_of([cross], gram)
        other = send(gram, swap)
    update = newton_schulz(gram, other, direction)
    with jax.named_scope("update_gather"):
        _, *updates = all_gather(update, sizes, rest)
    new_moment = in_order(eight, rest)
    update = in_order(*updates, [new_moment])
    return (new_moment, update)


def solution(mesh):
    sizes = (mesh.shape["dp"], mesh.shape["zero"])
    return jax.shard_map(
        functools.partial(per_device, sizes),
        mesh=mesh,
        in_specs=(P("dp", None, None, "zero"), P(None, None, "zero"), P()),
        out_specs=(P(None, None, "zero"), P(None, None, "zero")),
        check_vma=False,
    )
```
